32 devices in a mesh: dp: 8 (over y, x, core), shard: 4 (over z).
Axes of the slice: x: 2, y: 2, z: 4, core: 2. Of those that a mesh axis runs over, the one named last changes fastest.
Arguments:
- tokens: bfloat16 [49152, 576], P(('dp', 'shard')), may hold values from -6 to 6
- segments: int32 [49152], P(('dp', 'shard')), may hold values from 0 to 7, as said below
- norm_attn: bfloat16 [576], P('shard'), may hold values from 0.5 to 1.5
- w_query: bfloat16 [576, 576], P('shard'), may hold values from -0.25 to 0.25
- w_key: bfloat16 [576, 192], P('shard'), may hold values from -0.25 to 0.25
- w_value: bfloat16 [576, 192], P('shard'), may hold values from -0.25 to 0.25
- w_out: bfloat16 [576, 576], P('shard'), may hold values from -1 to 1
- norm_ffn: bfloat16 [576], P('shard'), may hold values from 0.5 to 1.5
- w_gate: bfloat16 [576, 1536], P('shard'), may hold values from -0.25 to 0.25
- w_up: bfloat16 [576, 1536], P('shard'), may hold values from -0.25 to 0.25
- w_down: bfloat16 [1536, 576], P('shard'), may hold values from -0.15625 to 0.15625
- cotangent: bfloat16 [49152, 576], P(('dp', 'shard')), may hold values from -6 to 6
Outputs:
- output: bfloat16 [49152, 576], P(('dp', 'shard'))
- input_grad: bfloat16 [49152, 576], P(('dp', 'shard'))
- grad_norm_attn: float32 [576], P('shard')
- grad_query: float32 [576, 576], P('shard')
- grad_key: float32 [576, 192], P('shard')
- grad_value: float32 [576, 192], P('shard')
- grad_out: float32 [576, 576], P('shard')
- grad_norm_ffn: float32 [576], P('shard')
- grad_gate: float32 [576, 1536], P('shard')
- grad_up: float32 [576, 1536], P('shard')
- grad_down: float32 [1536, 576], P('shard')
The draws below stay inside these ranges and needn't reach their ends.
Inputs may be any that keep to these rules, and one draw needn't show every extreme that they name: `segments`: within each aligned block of 512 tokens the segment ids begin at 0 and never fall; every fourth block is one sequence of 512 tokens.
All inputs are finite; a program needn't handle non-finite values.
Results may differ from the reference program's by a relative error of at most 0.012.
Values may be sent and summed in bfloat16 or wider, within the bound.
A program may use at most 192 MiB of HBM per device.

```python
import jax
import jax.numpy as jnp
from jax import lax

D = 576
HQ = 9
KVH = 3
HD = 64
FF = 1536
BLOCK = 512
TOK_DEV = 1536
TOKENS = 49152


def draw_segments(key, part):
    key = jax.random.fold_in(key, 11)
    blocks = TOKENS // BLOCK
    cut_points = jax.random.randint(key, (blocks, 7), 1, BLOCK)
    whole_block = (jnp.arange(blocks) % 4 == 0)[:, None]
    cut_points = jnp.where(whole_block, BLOCK, cut_points)
    slot_index = jnp.arange(BLOCK)
    counted = jnp.sum((cut_points[:, None, :] <= slot_index[None, :, None]).astype(jnp.int32), axis=-1)
    return counted.astype(jnp.int32).reshape(TOKENS)


def block_scale(rng, extent, cuts, least, largest):
    def one(dim, parts):
        draws = jax.random.uniform(jax.random.fold_in(jax.random.fold_in(rng, 6), dim), (parts,), jnp.float32, least / len(cuts), largest / len(cuts))
        return jnp.repeat(jnp.exp(draws), extent[dim] // parts).reshape((-1,) + (1,) * (len(extent) - dim - 1))

    gain = one(*cuts[0])
    for cut in cuts[1:]:
        gain = gain * one(*cut)
    return gain


def scatter_about(own_key, shape, deviation, reach, cuts=(), kind=jnp.bfloat16):
    drawn = jax.random.normal(own_key, shape, jnp.float32) * deviation
    if len(cuts) > 0:
        drawn = block_scale(own_key, shape, cuts, -0.22, 0.18) * drawn
    return jnp.clip(drawn, min=-reach, max=reach).astype(kind)


def setup_inputs(seed: int = 0) -> dict:
    streams_of = jax.random.split(jax.random.key(seed), 13)
    tokens = scatter_about(streams_of[0], (TOKENS, D), 1.0, 6.0, ((0, 32),))
    segments = draw_segments(jax.random.fold_in(streams_of[12], 71), 0)
    norm_attn = jnp.clip(1.0 + 0.1 * jax.random.normal(streams_of[2], (D,), jnp.float32), 0.5, 1.5).astype(jnp.bfloat16)
    w_query = scatter_about(streams_of[3], (D, D), D ** -0.5, 0.25, ((0, 4),))
    w_key = scatter_about(streams_of[4], (D, KVH * HD), D ** -0.5, 0.25, ((0, 4),))
    w_value = scatter_about(streams_of[5], (D, KVH * HD), D ** -0.5, 0.25, ((0, 4),))
    w_out = scatter_about(streams_of[6], (D, D), (D // 16) ** -0.5, 1.0, ((0, 4),))
    norm_ffn = jnp.clip(1.0 + 0.1 * jax.random.normal(streams_of[7], (D,), jnp.float32), 0.5, 1.5).astype(jnp.bfloat16)
    w_gate = scatter_about(streams_of[8], (D, FF), D ** -0.5, 0.25, ((0, 4),))
    w_up = scatter_about(streams_of[9], (D, FF), D ** -0.5, 0.25, ((0, 4),))
    w_down = scatter_about(streams_of[10], (FF, D), FF ** -0.5, 0.15625, ((0, 4),))
    cotangent = scatter_about(streams_of[11], (TOKENS, D), 1.0, 6.0, ((0, 32),))
    return dict(tokens=tokens, segments=segments, norm_attn=norm_attn, w_query=w_query, w_key=w_key, w_value=w_value, w_out=w_out, norm_ffn=norm_ffn, w_gate=w_gate, w_up=w_up, w_down=w_down, cotangent=cotangent)


precise = lax.Precision.HIGHEST
epsilon = 1e-05

@jax.custom_vjp
def low(v):
    return lax.optimization_barrier(v.astype(jnp.bfloat16)).astype(jnp.float32)

@jax.custom_vjp
def low_back(v):
    return v

def low_keep(v):
    return (low(v), None)

def low_pass(kept, grad):
    return (grad,)

def back_keep(v):
    return (v, None)

def back_low(kept, grad):
    return (low(grad),)
low.defvjp(low_keep, low_pass)
low_back.defvjp(back_keep, back_low)

def rms_scale(values, scales):
    return values * lax.rsqrt(lax.optimization_barrier(jnp.mean(values * values, axis=-1, keepdims=True)) + epsilon) * scales

def places_of(segment_ids):
    slot_index = jnp.arange(BLOCK, dtype=jnp.int32)
    earlier = jnp.concatenate([segment_ids[:, :1] - 1, segment_ids[:, :-1]], axis=1)
    starts = jnp.where(segment_ids != earlier, slot_index[None, :], 0)
    return (slot_index[None, :] - lax.cummax(starts, axis=1)).astype(jnp.float32)

def rope_tables(places):
    frequency = 100000.0 ** (jnp.arange(HD // 2, dtype=jnp.float32) * (-2.0 / HD))
    angles = places[..., None] * frequency
    angles = jnp.concatenate([angles, angles], axis=-1)
    return (jnp.cos(angles)[..., None, :], jnp.sin(angles)[..., None, :])

def rotate(values, cosine, sine_table):
    half_size = values.shape[-1] // 2
    turned = jnp.concatenate([-values[..., half_size:], values[..., :half_size]], axis=-1)
    return values * cosine + turned * sine_table

def layer(inputs, gain_one, query_w, key_w, value_w, out_w, gain_two, gate_w, up_w, down_w, cosine, sine_table, allowed):
    blocks = inputs.shape[0] // BLOCK
    normed_one = low(rms_scale(inputs, gain_one))
    queries = low_back(jnp.dot(normed_one, query_w, precision=precise)).reshape(blocks, BLOCK, HQ, HD)
    keys_raw = low_back(jnp.dot(normed_one, key_w, precision=precise)).reshape(blocks, BLOCK, KVH, HD)
    values = low(low_back(jnp.dot(normed_one, value_w, precision=precise))).reshape(blocks, BLOCK, KVH, HD)
    queries = low(rotate(queries, cosine, sine_table)).reshape(blocks, BLOCK, KVH, HQ // KVH, HD)
    keys_rot = low(rotate(keys_raw, cosine, sine_table))
    scores = jnp.einsum('bqkgd,bpkd->bkgqp', queries, keys_rot, precision=precise) * HD ** (-0.5)
    scores = low_back(jnp.where(allowed[:, None, None], scores, -1e+30))
    highest = lax.optimization_barrier(jnp.max(scores, axis=-1, keepdims=True))
    exponents = jnp.exp(scores - highest)
    probs_all = exponents / lax.optimization_barrier(jnp.sum(exponents, axis=-1, keepdims=True))
    mixed_heads = jnp.einsum('bkgqp,bpkd->bqkgd', low(probs_all), values, precision=precise)
    mixed_heads = low(low_back(mixed_heads.reshape(blocks * BLOCK, D)))
    middle = inputs + low_back(jnp.dot(mixed_heads, out_w, precision=precise))
    normed_two = low(rms_scale(middle, gain_two))
    gate_values = low_back(jnp.dot(normed_two, gate_w, precision=precise))
    upward = low_back(jnp.dot(normed_two, up_w, precision=precise))
    hidden = low(jax.nn.silu(gate_values) * upward)
    return middle + low_back(jnp.dot(hidden, down_w, precision=precise))

def reference(tokens, segments, norm_attn, w_query, w_key, w_value, w_out, norm_ffn, w_gate, w_up, w_down, cotangent):
    weights = tuple((w.astype(jnp.float32) for w in (norm_attn, w_query, w_key, w_value, w_out, norm_ffn, w_gate, w_up, w_down)))
    groups = TOKENS // TOK_DEV
    inputs_all = tokens.astype(jnp.float32).reshape(groups, TOK_DEV, D)
    segment_all = segments.reshape(groups, TOK_DEV // BLOCK, BLOCK)
    cotan_all = cotangent.astype(jnp.float32).reshape(groups, TOK_DEV, D)
    slot_index = jnp.arange(BLOCK, dtype=jnp.int32)

    def step_group(running, item):
        inputs, segment_ids, cotan_rows = item
        cosine, sine_table = rope_tables(places_of(segment_ids))
        allowed = (segment_ids[:, :, None] == segment_ids[:, None, :]) & (slot_index[:, None] >= slot_index[None, :])

        def forward(inputs_now, *params):
            return layer(inputs_now, *params, cosine, sine_table, allowed)
        result, pullback = jax.vjp(forward, inputs, *weights)
        gradient = pullback(cotan_rows)
        running = tuple((a + b for a, b in zip(running, gradient[1:])))
        return (running, (result.astype(jnp.bfloat16), gradient[0].astype(jnp.bfloat16)))
    zeros = tuple((jnp.zeros_like(w) for w in weights))
    running, (results, input_grads) = lax.scan(step_group, zeros, (inputs_all, segment_all, cotan_all))
    return (results.reshape(TOKENS, D), input_grads.reshape(TOKENS, D), running[0], running[1], running[2], running[3], running[4], running[5], running[6], running[7], running[8])
```

```python
import functools

import jax
import jax.numpy as jnp
from jax import lax
from jax.experimental import pallas as pl
from jax.experimental.pallas import tpu as pltpu
from jax.sharding import PartitionSpec as P

HQ = 9
KVH = 3
HD = 64
BLOCK = 512
HALF = 256
SLOT = 128
GROUPS = HQ // KVH
EPS = 1e-05
FAR = -1e30
VMEM_BYTES = 56 * 1024 * 1024

f32 = jnp.float32
bf16 = jnp.bfloat16


def dot(a, b):
    return lax.dot_general(a, b, (((1,), (0,)), ((), ())), preferred_element_type=f32)


def dot_t(a, b):
    return lax.dot_general(a, b, (((1,), (1,)), ((), ())), preferred_element_type=f32)


def slot(h):
    return pl.ds(pl.multiple_of(h * SLOT, SLOT), SLOT)


def split3(v):
    hi = v.astype(bf16).astype(f32)
    rest = v - hi
    mid = rest.astype(bf16).astype(f32)
    return hi, mid, rest - mid


def roll_half(v):
    return pltpu.roll(v, SLOT // 2, 1)


def attn_fwd(tok, cs, seg, gain, wqkv, q_out, k_out, v_out, mixed_out):
    x = tok[...].astype(f32)
    inv = lax.rsqrt(jnp.mean(x * x, axis=1, keepdims=True) + EPS)
    n = (x * inv * gain[...]).astype(bf16)
    lane = lax.broadcasted_iota(jnp.int32, (BLOCK, SLOT), 1)
    low = lane < HD
    same = (lane - 72) == seg[...]
    q_ext = jnp.where((lane >= 72) & (lane < 80) & jnp.logical_not(same), FAR, 0.0)
    k_ext = jnp.where(same | ((lane >= 64) & (lane < 67)), 1.0, 0.0)
    table = cs[...]
    for g in range(KVH):
        base = g * GROUPS * SLOT
        raw = dot(n, wqkv[:, base : base + GROUPS * SLOT])
        for j in range(GROUPS):
            r = raw[:, j * SLOT : (j + 1) * SLOT] * table
            r = (r + roll_half(r)) * (HD ** -0.5)
            q_out[:, base + j * SLOT : base + (j + 1) * SLOT] = jnp.where(low, r, q_ext).astype(bf16)
    raw = dot(n, wqkv[:, HQ * SLOT : (HQ + KVH) * SLOT])
    for g in range(KVH):
        r = raw[:, g * SLOT : (g + 1) * SLOT] * table
        r = r + roll_half(r)
        k_out[:, g * SLOT : (g + 1) * SLOT] = jnp.where(low, r, k_ext).astype(bf16)
    raw = dot(n, wqkv[:, (HQ + KVH) * SLOT :])
    for g in range(KVH):
        v_out[:, g * SLOT : (g + 1) * SLOT] = jnp.where(low, raw[:, g * SLOT : (g + 1) * SLOT], 1.0).astype(bf16)

    lane_h = lax.broadcasted_iota(jnp.int32, (HALF, SLOT), 1)
    low_h = lane_h < HD

    def group(g, carry):
        for j in range(GROUPS):
            h = g * GROUPS + j
            for i in range(2):
                rows = slice(i * HALF, (i + 1) * HALF)
                width = (i + 1) * HALF
                q = q_out[rows, slot(h)]
                s = dot_t(q, k_out[:width, slot(g)])
                seen = (
                    lax.broadcasted_iota(jnp.int32, (HALF, width), 0) + i * HALF
                    >= lax.broadcasted_iota(jnp.int32, (HALF, width), 1)
                )
                s = jnp.where(seen, s, FAR)
                m = jnp.max(s, axis=1, keepdims=True)
                e = jnp.exp(s - m).astype(bf16)
                r = dot(e, v_out[:width, slot(g)])
                total = jnp.where(low_h, roll_half(r), r)
                mixed_out[rows, slot(h)] = jnp.where(low_h, r / total, 0.0).astype(bf16)
                hi, mid, lo = split3(m + jnp.log(total))
                q = jnp.where(lane_h == 64, -hi, q.astype(f32))
                q = jnp.where(lane_h == 65, -mid, q)
                q = jnp.where(lane_h == 66, -lo, q)
                q_out[rows, slot(h)] = q.astype(bf16)
        return carry

    lax.fori_loop(0, KVH, group, 0)


def norm_back(g, x, inv, gain):
    u = g * gain
    part = inv * (u - x * (inv * inv) * jnp.mean(u * x, axis=1, keepdims=True))
    return part, jnp.sum(g * x * inv, axis=0, keepdims=True)


CHUNK = 512


def ffn(tok, mixed, cot, gain, wout, wg, wu, wd, out, mgrad, xgrad, dout, dg, du, dd, dgain, n2, n2t, cott, acc, back):
    @pl.when(pl.program_id(0) == 0)
    def _():
        dout[...] = jnp.zeros_like(dout)
        dg[...] = jnp.zeros_like(dg)
        du[...] = jnp.zeros_like(du)
        dd[...] = jnp.zeros_like(dd)
        dgain[...] = jnp.zeros_like(dgain)

    middle = tok[...].astype(f32) + dot(mixed[...], wout[...])
    inv = lax.rsqrt(jnp.mean(middle * middle, axis=1, keepdims=True) + EPS)
    normed = middle * inv * gain[...]
    n2[...] = normed.astype(bf16)
    n2t[...] = normed.T.astype(bf16)
    cott[...] = cot[...].astype(f32).T.astype(bf16)
    acc[...] = middle
    back[...] = jnp.zeros_like(back)

    def step(c, carry):
        part = pl.ds(pl.multiple_of(c * CHUNK, CHUNK), CHUNK)
        a = dot(n2[...], wg[:, part])
        b = dot(n2[...], wu[:, part])
        s = jax.nn.sigmoid(a)
        silu = a * s
        h = (silu * b).astype(bf16)
        hg = dot_t(cot[...], wd[part, :])
        ga = (hg * b * (s * (1.0 + a * (1.0 - s)))).astype(bf16)
        ub = (hg * silu).astype(bf16)
        acc[...] += dot(h, wd[part, :])
        dd[:, part] += dot(cott[...], h)
        dg[:, part] += dot(n2t[...], ga)
        du[:, part] += dot(n2t[...], ub)
        back[...] += dot_t(ga, wg[:, part]) + dot_t(ub, wu[:, part])
        return carry

    lax.fori_loop(0, wg.shape[1] // CHUNK, step, 0)
    out[...] = acc[...].astype(bf16)
    middle = tok[...].astype(f32) + dot(mixed[...], wout[...])
    inv = lax.rsqrt(jnp.mean(middle * middle, axis=1, keepdims=True) + EPS)
    part, gain_part = norm_back(back[...], middle, inv, gain[...])
    dgain[...] += gain_part
    total = cot[...].astype(f32) + part
    mgrad[...] = total
    branch = total.astype(bf16)
    xgrad[...] = dot_t(branch, wout[...]).astype(bf16)
    dout[...] += dot(mixed[...].astype(f32).T.astype(bf16), branch)


def attn_bwd(tok, cs, gain, wqkv, q_in, k_in, v_in, mixed, xgrad, mgrad, igrad, dw, dgain, dpad):
    @pl.when(pl.program_id(0) == 0)
    def _():
        dw[...] = jnp.zeros_like(dw)
        dgain[...] = jnp.zeros_like(dgain)

    lane = lax.broadcasted_iota(jnp.int32, (BLOCK, SLOT), 1)
    low = lane < HD
    table = cs[...]
    wide_seen = lax.broadcasted_iota(jnp.int32, (HALF, BLOCK), 0) <= lax.broadcasted_iota(jnp.int32, (HALF, BLOCK), 1)
    near_seen = wide_seen[:, :HALF]

    def group(g, carry):
        k = k_in[:, slot(g)]
        v = v_in[:, slot(g)]
        kt = k.astype(f32).T.astype(bf16)
        dk0 = dv0 = dk1 = dv1 = None
        for j in range(GROUPS):
            h = g * GROUPS + j
            q = q_in[:, slot(h)]
            go = xgrad[:, slot(h)].astype(f32)
            delta = jnp.sum(go * mixed[:, slot(h)].astype(f32), axis=1, keepdims=True)
            hi, mid, lo = split3(delta)
            go = jnp.where(lane == 64, -hi, go)
            go = jnp.where(lane == 65, -mid, go)
            go = jnp.where(lane == 66, -lo, go).astype(bf16)
            p0 = jnp.exp(jnp.where(wide_seen, dot_t(k[:HALF], q), FAR))
            s0 = (p0 * dot_t(v[:HALF], go)).astype(bf16)
            dv = dot(p0.astype(bf16), go)
            dk = dot(s0, q)
            dv0 = dv if dv0 is None else dv0 + dv
            dk0 = dk if dk0 is None else dk0 + dk
            p1 = jnp.exp(jnp.where(near_seen, dot_t(k[HALF:], q[HALF:]), FAR))
            s1 = (p1 * dot_t(v[HALF:], go[HALF:])).astype(bf16)
            dv = dot(p1.astype(bf16), go[HALF:])
            dk = dot(s1, q[HALF:])
            dv1 = dv if dv1 is None else dv1 + dv
            dk1 = dk if dk1 is None else dk1 + dk
            first = dot(kt[:, :HALF], s0)
            near = first[:, :HALF].T
            far = (first[:, HALF:] + dot(kt[:, HALF:], s1)).T
            dq = jnp.concatenate([near, far], axis=0) * (HD ** -0.5)
            dq = jnp.where(low, dq, 0.0)
            dpad[:, slot(h)] = ((dq + roll_half(dq)) * table).astype(bf16)
        dk = jnp.where(low, jnp.concatenate([dk0, dk1], axis=0), 0.0)
        dpad[:, slot(HQ + g)] = ((dk + roll_half(dk)) * table).astype(bf16)
        dv = jnp.where(low, jnp.concatenate([dv0, dv1], axis=0), 0.0)
        dpad[:, slot(HQ + KVH + g)] = dv.astype(bf16)
        return carry

    lax.fori_loop(0, KVH, group, 0)
    x = tok[...].astype(f32)
    inv = lax.rsqrt(jnp.mean(x * x, axis=1, keepdims=True) + EPS)
    nt = (x * inv * gain[...]).T.astype(bf16)
    dw[...] += dot(nt, dpad[...])
    part, gain_part = norm_back(dot_t(dpad[...], wqkv[...]), x, inv, gain[...])
    dgain[...] += gain_part
    igrad[...] = (mgrad[...] + part).astype(bf16)


def rows_spec(width):
    return pl.BlockSpec((BLOCK, width), lambda i: (i, 0))


def whole_spec(shape):
    return pl.BlockSpec(shape, lambda i: (0, 0), pipeline_mode=pl.Buffered(1))


def sum_spec(shape):
    return pl.BlockSpec(shape, lambda i: (0, 0))


def params():
    return pltpu.CompilerParams(vmem_limit_bytes=VMEM_BYTES, dimension_semantics=("arbitrary",))


def turned(w):
    half = HD // 2
    return jnp.concatenate([-w[..., half:], w[..., :half]], axis=-1)


def unturned(w):
    half = HD // 2
    return jnp.concatenate([w[..., half:], -w[..., :half]], axis=-1)


def tables_of(segments):
    rows = segments.shape[0]
    ids = segments.reshape(rows // BLOCK, BLOCK)
    index = jnp.arange(BLOCK, dtype=jnp.int32)
    earlier = jnp.concatenate([ids[:, :1] - 1, ids[:, :-1]], axis=1)
    starts = jnp.where(ids != earlier, index[None, :], 0)
    places = (index[None, :] - lax.cummax(starts, axis=1)).astype(f32).reshape(rows, 1)
    frequency = 100000.0 ** (jnp.arange(HD // 2, dtype=f32) * (-2.0 / HD))
    angles = places * frequency
    cosine, sine = jnp.cos(angles), jnp.sin(angles)
    return jnp.concatenate([cosine, cosine, sine, sine], axis=1)


def gather_weights(norm_attn, w_query, w_key, w_value, w_out, norm_ffn, w_gate, w_up, w_down):
    rows = norm_attn.shape[0]
    gains = jnp.concatenate(
        [norm_attn[:, None], norm_ffn[:, None], jnp.zeros((rows, SLOT - 2), bf16)], axis=1
    )
    down = w_down.reshape(rows, -1)
    packed = jnp.concatenate([w_gate, w_up, w_query, w_key, w_value, w_out, gains, down], axis=1)
    full = lax.all_gather(packed, "shard", axis=0, tiled=True)
    ff, d = w_gate.shape[1], w_query.shape[1]
    at = 2 * ff
    qk = full[:, at : at + (HQ + KVH) * HD]
    at += (HQ + KVH) * HD
    wv = full[:, at : at + KVH * HD]
    at += KVH * HD
    wout = full[:, at : at + d]
    at += d
    gain_one = full[:, at].astype(f32)[None, :]
    gain_two = full[:, at + 1].astype(f32)[None, :]
    at += SLOT
    wdown = full[:, at:].reshape(ff, d)
    return full[:, :ff], full[:, ff : 2 * ff], qk, wv, wout, gain_one, gain_two, wdown


def reduce_grads(by_columns):
    summed = lax.psum_scatter(by_columns, "shard", scatter_dimension=0, tiled=True)
    return lax.psum(summed, "dp").astype(f32)


def shards(tokens, segments, norm_attn, w_query, w_key, w_value, w_out, norm_ffn, w_gate, w_up, w_down, cotangent):
    rows, d = tokens.shape
    ff = w_gate.shape[1]
    nshard = d // norm_attn.shape[0]
    grid = (rows // BLOCK,)
    wg, wu, qk, wv, wout, gain_one, gain_two, wdown = gather_weights(
        norm_attn, w_query, w_key, w_value, w_out, norm_ffn, w_gate, w_up, w_down
    )
    qk = qk.reshape(d, HQ + KVH, HD)
    qk = jnp.concatenate([qk, turned(qk)], axis=-1).reshape(d, -1)
    wv = jnp.pad(wv.reshape(d, KVH, HD), ((0, 0), (0, 0), (0, SLOT - HD))).reshape(d, -1)
    wqkv = jnp.concatenate([qk, wv], axis=1)
    wout = jnp.pad(wout.reshape(HQ, HD, d), ((0, 0), (0, SLOT - HD), (0, 0))).reshape(HQ * SLOT, d)
    cs = tables_of(segments)
    seg = segments[:, None]
    qw, kw, allw = HQ * SLOT, KVH * SLOT, (HQ + 2 * KVH) * SLOT
    shape = jax.ShapeDtypeStruct

    q, k, v, mixed = pl.pallas_call(
        attn_fwd,
        grid=grid,
        in_specs=[rows_spec(d), rows_spec(SLOT), rows_spec(1), whole_spec((1, d)), whole_spec((d, allw))],
        out_specs=[rows_spec(qw), rows_spec(kw), rows_spec(kw), rows_spec(qw)],
        out_shape=[shape((rows, qw), bf16), shape((rows, kw), bf16), shape((rows, kw), bf16), shape((rows, qw), bf16)],
        compiler_params=params(),
        name="attn_fwd",
    )(tokens, cs, seg, gain_one, wqkv)

    output, mgrad, xgrad, dout, dg, du, dd, dgain_two = pl.pallas_call(
        ffn,
        grid=grid,
        in_specs=[
            rows_spec(d), rows_spec(qw), rows_spec(d), whole_spec((1, d)), whole_spec((qw, d)),
            whole_spec((d, ff)), whole_spec((d, ff)), whole_spec((ff, d)),
        ],
        out_specs=[
            rows_spec(d), rows_spec(d), rows_spec(qw), whole_spec((qw, d)), whole_spec((d, ff)),
            whole_spec((d, ff)), whole_spec((d, ff)), whole_spec((1, d)),
        ],
        out_shape=[
            shape((rows, d), bf16), shape((rows, d), f32), shape((rows, qw), bf16), shape((qw, d), f32),
            shape((d, ff), f32), shape((d, ff), f32), shape((d, ff), f32), shape((1, d), f32),
        ],
        scratch_shapes=[
            pltpu.VMEM((BLOCK, d), bf16), pltpu.VMEM((d, BLOCK), bf16), pltpu.VMEM((d, BLOCK), bf16),
            pltpu.VMEM((BLOCK, d), f32), pltpu.VMEM((BLOCK, d), f32),
        ],
        compiler_params=params(),
        name="ffn",
    )(tokens, mixed, cotangent, gain_two, wout, wg, wu, wdown)

    igrad, dw, dgain_one = pl.pallas_call(
        attn_bwd,
        grid=grid,
        in_specs=[
            rows_spec(d), rows_spec(SLOT), whole_spec((1, d)), whole_spec((d, allw)), rows_spec(qw),
            rows_spec(kw), rows_spec(kw), rows_spec(qw), rows_spec(qw), rows_spec(d),
        ],
        out_specs=[rows_spec(d), whole_spec((d, allw)), whole_spec((1, d))],
        out_shape=[shape((rows, d), bf16), shape((d, allw), f32), shape((1, d), f32)],
        scratch_shapes=[pltpu.VMEM((BLOCK, allw), bf16)],
        compiler_params=params(),
        name="attn_bwd",
    )(tokens, cs, gain_one, wqkv, q, k, v, mixed, xgrad, mgrad)

    dqk = dw[:, : (HQ + KVH) * SLOT].reshape(d, HQ + KVH, SLOT)
    dqk = (dqk[..., :HD] + unturned(dqk[..., HD:])).reshape(d, -1)
    dv = dw[:, (HQ + KVH) * SLOT :].reshape(d, KVH, SLOT)[..., :HD].reshape(d, -1)
    dout = dout.reshape(HQ, SLOT, d)[:, :HD].reshape(d, d)
    own_ff = ff // nshard
    dd = dd.reshape(d, nshard, own_ff).transpose(1, 0, 2).reshape(nshard * own_ff, d)
    dd = dd.reshape(d, ff)
    first = jnp.concatenate([dg.astype(bf16), du.astype(bf16), dd.astype(bf16)], axis=1)
    gains = jnp.concatenate([dgain_one.T, dgain_two.T, jnp.zeros((d, SLOT - 2), f32)], axis=1)
    second = jnp.concatenate([dqk, dv, dout, gains], axis=1).astype(bf16)
    first = reduce_grads(first)
    second = reduce_grads(second)
    own_d = d // nshard
    down = first[:, 2 * ff :].reshape(d, own_ff).T
    nq, nk = HQ * HD, KVH * HD
    at = nq + 2 * nk
    return (
        output,
        igrad,
        second[:, at + d],
        second[:, :nq],
        second[:, nq : nq + nk],
        second[:, nq + nk : at],
        second[:, at : at + d],
        second[:, at + d + 1],
        first[:, :ff],
        first[:, ff : 2 * ff],
        down,
    )


def solution(mesh):
    rows = P(("dp", "shard"), None)
    weight, gain = P("shard", None), P("shard")
    in_specs = (
        rows, P(("dp", "shard")), gain, weight, weight, weight, weight, gain, weight, weight, weight, rows
    )
    out_specs = (rows, rows, gain, weight, weight, weight, weight, gain, weight, weight, weight)
    return jax.shard_map(shards, mesh=mesh, in_specs=in_specs, out_specs=out_specs, check_vma=False)
```

```python
import functools

import jax
import jax.numpy as jnp
from jax import lax
from jax.experimental import pallas as pl
from jax.experimental.pallas import tpu as pltpu
from jax.sharding import PartitionSpec as P

HQ = 9
KVH = 3
HD = 64
BLOCK = 512
HALF = 256
SLOT = 128
GROUPS = HQ // KVH
EPS = 1e-05
FAR = -1e30
VMEM_BYTES = 56 * 1024 * 1024

f32 = jnp.float32
bf16 = jnp.bfloat16


def dot(a, b):
    return lax.dot_general(a, b, (((1,), (0,)), ((), ())), preferred_element_type=f32)


def dot_t(a, b):
    return lax.dot_general(a, b, (((1,), (1,)), ((), ())), preferred_element_type=f32)


def slot(h):
    return pl.ds(pl.multiple_of(h * SLOT, SLOT), SLOT)


def split3(v):
    hi = v.astype(bf16).astype(f32)
    rest = v - hi
    mid = rest.astype(bf16).astype(f32)
    return hi, mid, rest - mid


def roll_half(v):
    return pltpu.roll(v, SLOT // 2, 1)


def attn_fwd(tok, cs, seg, gain, wqkv, q_out, k_out, v_out, mixed_out):
    x = tok[...].astype(f32)
    inv = lax.rsqrt(jnp.mean(x * x, axis=1, keepdims=True) + EPS)
    n = (x * inv * gain[...]).astype(bf16)
    lane = lax.broadcasted_iota(jnp.int32, (BLOCK, SLOT), 1)
    low = lane < HD
    same = (lane - 72) == seg[...]
    q_ext = jnp.where((lane >= 72) & (lane < 80) & jnp.logical_not(same), FAR, 0.0)
    k_ext = jnp.where(same | ((lane >= 64) & (lane < 67)), 1.0, 0.0)
    table = cs[...]
    for g in range(KVH):
        base = g * GROUPS * SLOT
        raw = dot(n, wqkv[:, base : base + GROUPS * SLOT])
        for j in range(GROUPS):
            r = raw[:, j * SLOT : (j + 1) * SLOT] * table
            r = (r + roll_half(r)) * (HD ** -0.5)
            q_out[:, base + j * SLOT : base + (j + 1) * SLOT] = jnp.where(low, r, q_ext).astype(bf16)
    raw = dot(n, wqkv[:, HQ * SLOT : (HQ + KVH) * SLOT])
    for g in range(KVH):
        r = raw[:, g * SLOT : (g + 1) * SLOT] * table
        r = r + roll_half(r)
        k_out[:, g * SLOT : (g + 1) * SLOT] = jnp.where(low, r, k_ext).astype(bf16)
    raw = dot(n, wqkv[:, (HQ + KVH) * SLOT :])
    for g in range(KVH):
        v_out[:, g * SLOT : (g + 1) * SLOT] = jnp.where(low, raw[:, g * SLOT : (g + 1) * SLOT], 1.0).astype(bf16)

    lane_h = lax.broadcasted_iota(jnp.int32, (HALF, SLOT), 1)
    low_h = lane_h < HD

    def group(g, carry):
        for j in range(GROUPS):
            h = g * GROUPS + j
            for i in range(2):
                rows = slice(i * HALF, (i + 1) * HALF)
                width = (i + 1) * HALF
                q = q_out[rows, slot(h)]
                s = dot_t(q, k_out[:width, slot(g)])
                seen = (
                    lax.broadcasted_iota(jnp.int32, (HALF, width), 0) + i * HALF
                    >= lax.broadcasted_iota(jnp.int32, (HALF, width), 1)
                )
                s = jnp.where(seen, s, FAR)
                m = jnp.max(s, axis=1, keepdims=True)
                e = jnp.exp(s - m).astype(bf16)
                r = dot(e, v_out[:width, slot(g)])
                total = jnp.where(low_h, roll_half(r), r)
                mixed_out[rows, slot(h)] = jnp.where(low_h, r / total, 0.0).astype(bf16)
                hi, mid, lo = split3(m + jnp.log(total))
                q = jnp.where(lane_h == 64, -hi, q.astype(f32))
                q = jnp.where(lane_h == 65, -mid, q)
                q = jnp.where(lane_h == 66, -lo, q)
                q_out[rows, slot(h)] = q.astype(bf16)
        return carry

    lax.fori_loop(0, KVH, group, 0)


def norm_back(g, x, inv, gain):
    u = g * gain
    part = inv * (u - x * (inv * inv) * jnp.mean(u * x, axis=1, keepdims=True))
    return part, jnp.sum(g * x * inv, axis=0, keepdims=True)


CHUNK = 512


def ffn(tok, mixed, cot, gain, wout, wg, wu, wd, out, mgrad, xgrad, dout, dg, du, dd, dgain, n2, n2t, cott, acc, back):
    @pl.when(pl.program_id(0) == 0)
    def _():
        dout[...] = jnp.zeros_like(dout)
        dg[...] = jnp.zeros_like(dg)
        du[...] = jnp.zeros_like(du)
        dd[...] = jnp.zeros_like(dd)
        dgain[...] = jnp.zeros_like(dgain)

    middle = tok[...].astype(f32) + dot(mixed[...], wout[...])
    inv = lax.rsqrt(jnp.mean(middle * middle, axis=1, keepdims=True) + EPS)
    normed = middle * inv * gain[...]
    n2[...] = normed.astype(bf16)
    n2t[...] = normed.T.astype(bf16)
    cott[...] = cot[...].astype(f32).T.astype(bf16)
    acc[...] = middle
    back[...] = jnp.zeros_like(back)

    def step(c, carry):
        part = pl.ds(pl.multiple_of(c * CHUNK, CHUNK), CHUNK)
        a = dot(n2[...], wg[:, part])
        b = dot(n2[...], wu[:, part])
        s = jax.nn.sigmoid(a)
        silu = a * s
        h = (silu * b).astype(bf16)
        hg = dot_t(cot[...], wd[part, :])
        ga = (hg * b * (s * (1.0 + a * (1.0 - s)))).astype(bf16)
        ub = (hg * silu).astype(bf16)
        acc[...] += dot(h, wd[part, :])
        dd[:, part] += dot(cott[...], h)
        dg[:, part] += dot(n2t[...], ga)
        du[:, part] += dot(n2t[...], ub)
        back[...] += dot_t(ga, wg[:, part]) + dot_t(ub, wu[:, part])
        return carry

    lax.fori_loop(0, wg.shape[1] // CHUNK, step, 0)
    out[...] = acc[...].astype(bf16)
    middle = tok[...].astype(f32) + dot(mixed[...], wout[...])
    inv = lax.rsqrt(jnp.mean(middle * middle, axis=1, keepdims=True) + EPS)
    part, gain_part = norm_back(back[...], middle, inv, gain[...])
    dgain[...] += gain_part
    total = cot[...].astype(f32) + part
    mgrad[...] = total
    branch = total.astype(bf16)
    xgrad[...] = dot_t(branch, wout[...]).astype(bf16)
    dout[...] += dot(mixed[...].astype(f32).T.astype(bf16), branch)


def attn_bwd(tok, cs, gain, wqkv, q_in, k_in, v_in, mixed, xgrad, mgrad, igrad, dw, dgain, dpad):
    @pl.when(pl.program_id(0) == 0)
    def _():
        dw[...] = jnp.zeros_like(dw)
        dgain[...] = jnp.zeros_like(dgain)

    lane = lax.broadcasted_iota(jnp.int32, (BLOCK, SLOT), 1)
    low = lane < HD
    table = cs[...]
    wide_seen = lax.broadcasted_iota(jnp.int32, (HALF, BLOCK), 0) <= lax.broadcasted_iota(jnp.int32, (HALF, BLOCK), 1)
    near_seen = wide_seen[:, :HALF]

    def group(g, carry):
        k = k_in[:, slot(g)]
        v = v_in[:, slot(g)]
        kt = k.astype(f32).T.astype(bf16)
        dk0 = dv0 = dk1 = dv1 = None
        for j in range(GROUPS):
            h = g * GROUPS + j
            q = q_in[:, slot(h)]
            go = xgrad[:, slot(h)].astype(f32)
            delta = jnp.sum(go * mixed[:, slot(h)].astype(f32), axis=1, keepdims=True)
            hi, mid, lo = split3(delta)
            go = jnp.where(lane == 64, -hi, go)
            go = jnp.where(lane == 65, -mid, go)
            go = jnp.where(lane == 66, -lo, go).astype(bf16)
            p0 = jnp.exp(jnp.where(wide_seen, dot_t(k[:HALF], q), FAR))
            s0 = (p0 * dot_t(v[:HALF], go)).astype(bf16)
            dv = dot(p0.astype(bf16), go)
            dk = dot(s0, q)
            dv0 = dv if dv0 is None else dv0 + dv
            dk0 = dk if dk0 is None else dk0 + dk
            p1 = jnp.exp(jnp.where(near_seen, dot_t(k[HALF:], q[HALF:]), FAR))
            s1 = (p1 * dot_t(v[HALF:], go[HALF:])).astype(bf16)
            dv = dot(p1.astype(bf16), go[HALF:])
            dk = dot(s1, q[HALF:])
            dv1 = dv if dv1 is None else dv1 + dv
            dk1 = dk if dk1 is None else dk1 + dk
            first = dot(kt[:, :HALF], s0)
            near = first[:, :HALF].T
            far = (first[:, HALF:] + dot(kt[:, HALF:], s1)).T
            dq = jnp.concatenate([near, far], axis=0) * (HD ** -0.5)
            dq = jnp.where(low, dq, 0.0)
            dpad[:, slot(h)] = ((dq + roll_half(dq)) * table).astype(bf16)
        dk = jnp.where(low, jnp.concatenate([dk0, dk1], axis=0), 0.0)
        dpad[:, slot(HQ + g)] = ((dk + roll_half(dk)) * table).astype(bf16)
        dv = jnp.where(low, jnp.concatenate([dv0, dv1], axis=0), 0.0)
        dpad[:, slot(HQ + KVH + g)] = dv.astype(bf16)
        return carry

    lax.fori_loop(0, KVH, group, 0)
    x = tok[...].astype(f32)
    inv = lax.rsqrt(jnp.mean(x * x, axis=1, keepdims=True) + EPS)
    nt = (x * inv * gain[...]).T.astype(bf16)
    dw[...] += dot(nt, dpad[...])
    part, gain_part = norm_back(dot_t(dpad[...], wqkv[...]), x, inv, gain[...])
    dgain[...] += gain_part
    igrad[...] = (mgrad[...] + part).astype(bf16)


def rows_spec(width):
    return pl.BlockSpec((BLOCK, width), lambda i: (i, 0))


def whole_spec(shape):
    return pl.BlockSpec(shape, lambda i: (0, 0), pipeline_mode=pl.Buffered(1))


def sum_spec(shape):
    return pl.BlockSpec(shape, lambda i: (0, 0))


def params():
    return pltpu.CompilerParams(vmem_limit_bytes=VMEM_BYTES, dimension_semantics=("arbitrary",))


def turned(w):
    half = HD // 2
    return jnp.concatenate([-w[..., half:], w[..., :half]], axis=-1)


def unturned(w):
    half = HD // 2
    return jnp.concatenate([w[..., half:], -w[..., :half]], axis=-1)


def tables_of(segments):
    rows = segments.shape[0]
    ids = segments.reshape(rows // BLOCK, BLOCK)
    index = jnp.arange(BLOCK, dtype=jnp.int32)
    earlier = jnp.concatenate([ids[:, :1] - 1, ids[:, :-1]], axis=1)
    starts = jnp.where(ids != earlier, index[None, :], 0)
    places = (index[None, :] - lax.cummax(starts, axis=1)).astype(f32).reshape(rows, 1)
    frequency = 100000.0 ** (jnp.arange(HD // 2, dtype=f32) * (-2.0 / HD))
    angles = places * frequency
    cosine, sine = jnp.cos(angles), jnp.sin(angles)
    return jnp.concatenate([cosine, cosine, sine, sine], axis=1)


def partner_of(me, bit):
    value = (me // 2**bit) % 2
    return value, me + (1 - 2 * value) * 2**bit


def greet(me, z, nbits, nshard):
    barrier = pltpu.get_barrier_semaphore()
    for bit in range(nbits):
        pl.semaphore_signal(
            barrier, inc=1, device_id=(partner_of(me, bit)[1], z), device_id_type=pl.DeviceIdType.MESH
        )
    for t in range(1, nshard):
        pl.semaphore_signal(
            barrier, inc=1, device_id=(me, (z + t) % nshard), device_id_type=pl.DeviceIdType.MESH
        )
    pl.semaphore_wait(barrier, nbits + nshard - 1)


def send(src, dst, sems, index, dp_id, z_id):
    copy = pltpu.make_async_remote_copy(
        src_ref=src,
        dst_ref=dst,
        send_sem=sems[0].at[index],
        recv_sem=sems[1].at[index],
        device_id=(dp_id, z_id),
        device_id_type=pl.DeviceIdType.MESH,
    )
    copy.start()
    return copy


def take_turns(chains):
    chains = list(chains)
    while chains:
        left = []
        for chain in chains:
            if next(chain, None) is not None:
                left.append(chain)
        chains = left


def gather_chain(order, me, z, nshard, w, full, sems):
    panels = w.shape[0]
    size, lo = panels, 0
    for bit in order:
        size //= 2
        lo = lo + partner_of(me, bit)[0] * size
    copies = []
    for t in range(1, nshard):
        copies.append(
            send(w.at[pl.ds(lo, size)], full.at[pl.ds(lo, size), z], sems, t - 1, me, (z + t) % nshard)
        )

    def own(i, carry):
        full[i, z] = w[i]
        return carry

    lax.fori_loop(0, panels, own, 0)
    yield True
    for copy in copies:
        copy.wait()
    used = nshard - 1
    for bit in reversed(order):
        value, partner = partner_of(me, bit)
        copies = []
        for t in range(1, nshard):
            part = full.at[pl.ds(lo, size), (z + t) % nshard]
            copies.append(send(part, part, sems, used + t - 1, partner, z))
        used += nshard - 1
        yield True
        for copy in copies:
            copy.wait()
        lo = lo - value * size
        size *= 2


def gather_kernel(orders, nshard, w0, w1, f0, f1, s0, r0, s1, r1):
    me, z = lax.axis_index("dp"), lax.axis_index("shard")
    greet(me, z, len(orders[0]), nshard)
    take_turns(
        [
            gather_chain(orders[0], me, z, nshard, w0, f0, (s0, r0)),
            gather_chain(orders[1], me, z, nshard, w1, f1, (s1, r1)),
        ]
    )


def reduce_chain(order, me, z, nshard, x, out, acc, recv, pieces, sems):
    size = x.shape[0]
    lo, place, landing = 0, 0, 0
    for k, bit in enumerate(order):
        size //= 2
        value, partner = partner_of(me, bit)
        source = x if k == 0 else acc
        copy = send(
            source.at[pl.ds(lo + (1 - value) * size, size)], recv.at[pl.ds(landing, size)], sems, k, partner, z
        )
        yield True
        copy.wait()
        keep = lo + value * size
        target = 0 if k == 0 else keep

        def add(i, carry, source=source, keep=keep, target=target, landing=landing):
            acc[target + i] = (source[keep + i].astype(f32) + recv[landing + i].astype(f32)).astype(bf16)
            return carry

        lax.fori_loop(0, size, add, 0)
        lo = target
        place = place + value * size
        landing += size
    used = len(order)
    copies = []
    for t in range(1, nshard):
        there = (z + t) % nshard
        copies.append(send(acc.at[pl.ds(lo, size), there], pieces.at[t - 1], sems, used + t - 1, me, there))
    used += nshard - 1
    yield True
    for copy in copies:
        copy.wait()
    for i in range(size):
        total = acc[lo + i, z].astype(f32)
        for t in range(1, nshard):
            total = total + pieces[t - 1, i].astype(f32)
        out[place + i] = total.astype(bf16)
    for bit in reversed(order):
        value, partner = partner_of(me, bit)
        part = out.at[pl.ds(place, size)]
        copy = send(part, part, sems, used, partner, z)
        used += 1
        yield True
        copy.wait()
        place = place - value * size
        size *= 2


def reduce_kernel(orders, nshard, x0, x1, o0, o1, a0, r0, p0, a1, r1, p1, s0, t0, s1, t1):
    me, z = lax.axis_index("dp"), lax.axis_index("shard")
    greet(me, z, len(orders[0]), nshard)
    take_turns(
        [
            reduce_chain(orders[0], me, z, nshard, x0, o0, a0, r0, p0, (s0, t0)),
            reduce_chain(orders[1], me, z, nshard, x1, o1, a1, r1, p1, (s1, t1)),
        ]
    )


def orders_of(ndp):
    bits = list(range(ndp.bit_length() - 1))
    return bits, bits[:1] + bits[:0:-1]


def whole_vmem():
    return pl.BlockSpec(memory_space=pltpu.VMEM)


def gather_panels(ndp, nshard, w0, w1):
    rows = w0.shape[1]
    orders = orders_of(ndp)
    count = (nshard - 1) * (1 + len(orders[0]))
    return pl.pallas_call(
        functools.partial(gather_kernel, orders, nshard),
        in_specs=[whole_vmem()] * 2,
        out_specs=[whole_vmem()] * 2,
        out_shape=[jax.ShapeDtypeStruct((w.shape[0], nshard, rows, SLOT), bf16) for w in (w0, w1)],
        scratch_shapes=[pltpu.SemaphoreType.DMA((count,))] * 4,
        compiler_params=pltpu.CompilerParams(
            collective_id=0, has_side_effects=True, vmem_limit_bytes=VMEM_BYTES
        ),
        name="gather_panels",
    )(w0, w1)


def reduce_panels(ndp, nshard, x0, x1):
    rows = x0.shape[2]
    orders = orders_of(ndp)
    count = 2 * len(orders[0]) + nshard - 1
    scratch = []
    for x in (x0, x1):
        n = x.shape[0]
        scratch += [
            pltpu.VMEM((n // 2, nshard, rows, SLOT), bf16),
            pltpu.VMEM((n, nshard, rows, SLOT), bf16),
            pltpu.VMEM((nshard - 1, n // ndp, rows, SLOT), bf16),
        ]
    return pl.pallas_call(
        functools.partial(reduce_kernel, orders, nshard),
        in_specs=[whole_vmem()] * 2,
        out_specs=[whole_vmem()] * 2,
        out_shape=[jax.ShapeDtypeStruct((x.shape[0], rows, SLOT), bf16) for x in (x0, x1)],
        scratch_shapes=scratch + [pltpu.SemaphoreType.DMA((count,))] * 4,
        compiler_params=pltpu.CompilerParams(
            collective_id=1, has_side_effects=True, vmem_limit_bytes=VMEM_BYTES
        ),
        name="reduce_panels",
    )(x0, x1)


def to_panels(w, ndp):
    rows, columns = w.shape
    count = -(-columns // (SLOT * ndp)) * ndp
    w = jnp.pad(w, ((0, 0), (0, count * SLOT - columns)))
    return w.reshape(rows, count, SLOT).transpose(1, 0, 2)


def from_panels(p):
    return p.transpose(1, 0, 2).reshape(p.shape[1], -1)


def gather_weights(ndp, norm_attn, w_query, w_key, w_value, w_out, norm_ffn, w_gate, w_up, w_down):
    rows = norm_attn.shape[0]
    ff, d = w_gate.shape[1], w_query.shape[1]
    gains = jnp.concatenate(
        [norm_attn[:, None], norm_ffn[:, None], jnp.zeros((rows, HD - 2), bf16)], axis=1
    )
    down = w_down.reshape(rows, -1)
    first = to_panels(jnp.concatenate([w_gate, w_up], axis=1), ndp)
    second = to_panels(jnp.concatenate([down, w_query, w_key, w_value, w_out, gains], axis=1), ndp)
    first, second = gather_panels(ndp, d // rows, first, second)
    first = from_panels(first.reshape(-1, d, SLOT))
    full = from_panels(second.reshape(-1, d, SLOT))
    wdown = full[:, :ff].reshape(ff, d)
    at = ff
    qk = full[:, at : at + (HQ + KVH) * HD]
    at += (HQ + KVH) * HD
    wv = full[:, at : at + KVH * HD]
    at += KVH * HD
    wout = full[:, at : at + d]
    at += d
    gain_one = full[:, at].astype(f32)[None, :]
    gain_two = full[:, at + 1].astype(f32)[None, :]
    return first[:, :ff], first[:, ff : 2 * ff], qk, wv, wout, gain_one, gain_two, wdown


def shards(ndp, tokens, segments, norm_attn, w_query, w_key, w_value, w_out, norm_ffn, w_gate, w_up, w_down, cotangent):
    rows, d = tokens.shape
    ff = w_gate.shape[1]
    nshard = d // norm_attn.shape[0]
    grid = (rows // BLOCK,)
    wg, wu, qk, wv, wout, gain_one, gain_two, wdown = gather_weights(
        ndp, norm_attn, w_query, w_key, w_value, w_out, norm_ffn, w_gate, w_up, w_down
    )
    qk = qk.reshape(d, HQ + KVH, HD)
    qk = jnp.concatenate([qk, turned(qk)], axis=-1).reshape(d, -1)
    wv = jnp.pad(wv.reshape(d, KVH, HD), ((0, 0), (0, 0), (0, SLOT - HD))).reshape(d, -1)
    wqkv = jnp.concatenate([qk, wv], axis=1)
    wout = jnp.pad(wout.reshape(HQ, HD, d), ((0, 0), (0, SLOT - HD), (0, 0))).reshape(HQ * SLOT, d)
    cs = tables_of(segments)
    seg = segments[:, None]
    qw, kw, allw = HQ * SLOT, KVH * SLOT, (HQ + 2 * KVH) * SLOT
    shape = jax.ShapeDtypeStruct

    q, k, v, mixed = pl.pallas_call(
        attn_fwd,
        grid=grid,
        in_specs=[rows_spec(d), rows_spec(SLOT), rows_spec(1), whole_spec((1, d)), whole_spec((d, allw))],
        out_specs=[rows_spec(qw), rows_spec(kw), rows_spec(kw), rows_spec(qw)],
        out_shape=[shape((rows, qw), bf16), shape((rows, kw), bf16), shape((rows, kw), bf16), shape((rows, qw), bf16)],
        compiler_params=params(),
        name="attn_fwd",
    )(tokens, cs, seg, gain_one, wqkv)

    output, mgrad, xgrad, dout, dg, du, dd, dgain_two = pl.pallas_call(
        ffn,
        grid=grid,
        in_specs=[
            rows_spec(d), rows_spec(qw), rows_spec(d), whole_spec((1, d)), whole_spec((qw, d)),
            whole_spec((d, ff)), whole_spec((d, ff)), whole_spec((ff, d)),
        ],
        out_specs=[
            rows_spec(d), rows_spec(d), rows_spec(qw), whole_spec((qw, d)), whole_spec((d, ff)),
            whole_spec((d, ff)), whole_spec((d, ff)), whole_spec((1, d)),
        ],
        out_shape=[
            shape((rows, d), bf16), shape((rows, d), f32), shape((rows, qw), bf16), shape((qw, d), f32),
            shape((d, ff), f32), shape((d, ff), f32), shape((d, ff), f32), shape((1, d), f32),
        ],
        scratch_shapes=[
            pltpu.VMEM((BLOCK, d), bf16), pltpu.VMEM((d, BLOCK), bf16), pltpu.VMEM((d, BLOCK), bf16),
            pltpu.VMEM((BLOCK, d), f32), pltpu.VMEM((BLOCK, d), f32),
        ],
        compiler_params=params(),
        name="ffn",
    )(tokens, mixed, cotangent, gain_two, wout, wg, wu, wdown)

    igrad, dw, dgain_one = pl.pallas_call(
        attn_bwd,
        grid=grid,
        in_specs=[
            rows_spec(d), rows_spec(SLOT), whole_spec((1, d)), whole_spec((d, allw)), rows_spec(qw),
            rows_spec(kw), rows_spec(kw), rows_spec(qw), rows_spec(qw), rows_spec(d),
        ],
        out_specs=[rows_spec(d), whole_spec((d, allw)), whole_spec((1, d))],
        out_shape=[shape((rows, d), bf16), shape((d, allw), f32), shape((1, d), f32)],
        scratch_shapes=[pltpu.VMEM((BLOCK, allw), bf16)],
        compiler_params=params(),
        name="attn_bwd",
    )(tokens, cs, gain_one, wqkv, q, k, v, mixed, xgrad, mgrad)

    dqk = dw[:, : (HQ + KVH) * SLOT].reshape(d, HQ + KVH, SLOT)
    dqk = (dqk[..., :HD] + unturned(dqk[..., HD:])).reshape(d, -1)
    dv = dw[:, (HQ + KVH) * SLOT :].reshape(d, KVH, SLOT)[..., :HD].reshape(d, -1)
    dout = dout.reshape(HQ, SLOT, d)[:, :HD].reshape(d, d)
    own_ff = ff // nshard
    dd = dd.reshape(d, nshard, own_ff).transpose(1, 0, 2).reshape(nshard * own_ff, d)
    dd = dd.reshape(d, ff)
    gains = jnp.concatenate([dgain_one.T, dgain_two.T, jnp.zeros((d, HD - 2), f32)], axis=1)
    first = to_panels(jnp.concatenate([dg, du], axis=1).astype(bf16), ndp)
    second = to_panels(jnp.concatenate([dd, dqk, dv, dout, gains], axis=1).astype(bf16), ndp)
    first = first.reshape(-1, nshard, d // nshard, SLOT)
    second = second.reshape(-1, nshard, d // nshard, SLOT)
    first, second = reduce_panels(ndp, nshard, first, second)
    first = from_panels(first).astype(f32)
    second = from_panels(second).astype(f32)
    down = second[:, :ff].reshape(d, ff // nshard).T
    nq, nk = HQ * HD, KVH * HD
    second = second[:, ff:]
    at = nq + 2 * nk
    return (
        output,
        igrad,
        second[:, at + d],
        second[:, :nq],
        second[:, nq : nq + nk],
        second[:, nq + nk : at],
        second[:, at : at + d],
        second[:, at + d + 1],
        first[:, :ff],
        first[:, ff : 2 * ff],
        down,
    )


def solution(mesh):
    rows = P(("dp", "shard"), None)
    weight, gain = P("shard", None), P("shard")
    in_specs = (
        rows, P(("dp", "shard")), gain, weight, weight, weight, weight, gain, weight, weight, weight, rows
    )
    out_specs = (rows, rows, gain, weight, weight, weight, weight, gain, weight, weight, weight)
    return jax.shard_map(functools.partial(shards, mesh.shape["dp"]), mesh=mesh, in_specs=in_specs, out_specs=out_specs, check_vma=False)
```

```python
import functools

import jax
import jax.numpy as jnp
from jax import lax
from jax.experimental import pallas as pl
from jax.experimental.pallas import tpu as pltpu
from jax.sharding import PartitionSpec as P

HQ = 9
KVH = 3
HD = 64
BLOCK = 512
HALF = 256
SLOT = 128
GROUPS = HQ // KVH
EPS = 1e-05
FAR = -1e30
VMEM_BYTES = 56 * 1024 * 1024

f32 = jnp.float32
bf16 = jnp.bfloat16


def dot(a, b):
    return lax.dot_general(a, b, (((1,), (0,)), ((), ())), preferred_element_type=f32)


def dot_t(a, b):
    return lax.dot_general(a, b, (((1,), (1,)), ((), ())), preferred_element_type=f32)


def slot(h):
    return pl.ds(pl.multiple_of(h * SLOT, SLOT), SLOT)


def split3(v):
    hi = v.astype(bf16).astype(f32)
    rest = v - hi
    mid = rest.astype(bf16).astype(f32)
    return hi, mid, rest - mid


def roll_half(v):
    return pltpu.roll(v, SLOT // 2, 1)


def attn_fwd(tok, cs, seg, gain, wqkv, q_out, k_out, v_out, mixed_out):
    x = tok[...].astype(f32)
    inv = lax.rsqrt(jnp.mean(x * x, axis=1, keepdims=True) + EPS)
    n = (x * inv * gain[...]).astype(bf16)
    lane = lax.broadcasted_iota(jnp.int32, (BLOCK, SLOT), 1)
    low = lane < HD
    same = (lane - 72) == seg[...]
    q_ext = jnp.where((lane >= 72) & (lane < 80) & jnp.logical_not(same), FAR, 0.0)
    k_ext = jnp.where(same | ((lane >= 64) & (lane < 67)), 1.0, 0.0)
    table = cs[...]
    for g in range(KVH):
        base = g * GROUPS * SLOT
        raw = dot(n, wqkv[:, base : base + GROUPS * SLOT])
        for j in range(GROUPS):
            r = raw[:, j * SLOT : (j + 1) * SLOT] * table
            r = (r + roll_half(r)) * (HD ** -0.5)
            q_out[:, base + j * SLOT : base + (j + 1) * SLOT] = jnp.where(low, r, q_ext).astype(bf16)
    raw = dot(n, wqkv[:, HQ * SLOT : (HQ + KVH) * SLOT])
    for g in range(KVH):
        r = raw[:, g * SLOT : (g + 1) * SLOT] * table
        r = r + roll_half(r)
        k_out[:, g * SLOT : (g + 1) * SLOT] = jnp.where(low, r, k_ext).astype(bf16)
    raw = dot(n, wqkv[:, (HQ + KVH) * SLOT :])
    for g in range(KVH):
        v_out[:, g * SLOT : (g + 1) * SLOT] = jnp.where(low, raw[:, g * SLOT : (g + 1) * SLOT], 1.0).astype(bf16)

    lane_h = lax.broadcasted_iota(jnp.int32, (HALF, SLOT), 1)
    low_h = lane_h < HD

    def group(g, carry):
        for j in range(GROUPS):
            h = g * GROUPS + j
            for i in range(2):
                rows = slice(i * HALF, (i + 1) * HALF)
                width = (i + 1) * HALF
                q = q_out[rows, slot(h)]
                s = dot_t(q, k_out[:width, slot(g)])
                seen = (
                    lax.broadcasted_iota(jnp.int32, (HALF, width), 0) + i * HALF
                    >= lax.broadcasted_iota(jnp.int32, (HALF, width), 1)
                )
                s = jnp.where(seen, s, FAR)
                m = jnp.max(s, axis=1, keepdims=True)
                e = jnp.exp(s - m).astype(bf16)
                r = dot(e, v_out[:width, slot(g)])
                total = jnp.where(low_h, roll_half(r), r)
                mixed_out[rows, slot(h)] = jnp.where(low_h, r / total, 0.0).astype(bf16)
                hi, mid, lo = split3(m + jnp.log(total))
                q = jnp.where(lane_h == 64, -hi, q.astype(f32))
                q = jnp.where(lane_h == 65, -mid, q)
                q = jnp.where(lane_h == 66, -lo, q)
                q_out[rows, slot(h)] = q.astype(bf16)
        return carry

    lax.fori_loop(0, KVH, group, 0)


def norm_back(g, x, inv, gain):
    u = g * gain
    part = inv * (u - x * (inv * inv) * jnp.mean(u * x, axis=1, keepdims=True))
    return part, jnp.sum(g * x * inv, axis=0, keepdims=True)


CHUNK = 512


def emit(out, start, value):
    rows = out.shape[2]
    for z in range(out.shape[1]):
        out[start, z] = value[z * rows : (z + 1) * rows].astype(bf16)


def ffn(tok, mixed, cot, gain, wout, gu, wd, out, mgrad, xgrad, pout, pgu, dd, dgain, n2, n2t, cott, acc, back, wg, wu, dg, du, dout):
    tiles = wg.shape[1] // SLOT

    @pl.when(pl.program_id(0) == 0)
    def _():
        for p in range(tiles):
            wg[:, p * SLOT : (p + 1) * SLOT] = gu[p]
            wu[:, p * SLOT : (p + 1) * SLOT] = gu[tiles + p]
        dout[...] = jnp.zeros_like(dout)
        dg[...] = jnp.zeros_like(dg)
        du[...] = jnp.zeros_like(du)
        dd[...] = jnp.zeros_like(dd)
        dgain[...] = jnp.zeros_like(dgain)

    middle = tok[...].astype(f32) + dot(mixed[...], wout[...])
    inv = lax.rsqrt(jnp.mean(middle * middle, axis=1, keepdims=True) + EPS)
    normed = middle * inv * gain[...]
    n2[...] = normed.astype(bf16)
    n2t[...] = normed.T.astype(bf16)
    cott[...] = cot[...].astype(f32).T.astype(bf16)
    acc[...] = middle
    back[...] = jnp.zeros_like(back)

    def step(c, carry):
        part = pl.ds(pl.multiple_of(c * CHUNK, CHUNK), CHUNK)
        a = dot(n2[...], wg[:, part])
        b = dot(n2[...], wu[:, part])
        s = jax.nn.sigmoid(a)
        silu = a * s
        h = (silu * b).astype(bf16)
        hg = dot_t(cot[...], wd[part, :])
        ga = (hg * b * (s * (1.0 + a * (1.0 - s)))).astype(bf16)
        ub = (hg * silu).astype(bf16)
        acc[...] += dot(h, wd[part, :])
        dd[:, part] += dot(cott[...], h)
        dg[:, part] += dot(n2t[...], ga)
        du[:, part] += dot(n2t[...], ub)
        back[...] += dot_t(ga, wg[:, part]) + dot_t(ub, wu[:, part])
        return carry

    lax.fori_loop(0, wg.shape[1] // CHUNK, step, 0)
    out[...] = acc[...].astype(bf16)
    middle = tok[...].astype(f32) + dot(mixed[...], wout[...])
    inv = lax.rsqrt(jnp.mean(middle * middle, axis=1, keepdims=True) + EPS)
    part, gain_part = norm_back(back[...], middle, inv, gain[...])
    dgain[...] += gain_part
    total = cot[...].astype(f32) + part
    mgrad[...] = total
    branch = total.astype(bf16)
    xgrad[...] = dot_t(branch, wout[...]).astype(bf16)
    dout[...] += dot(mixed[...].astype(f32).T.astype(bf16), branch)

    @pl.when(pl.program_id(0) == pl.num_programs(0) - 1)
    def _():
        for p in range(tiles):
            emit(pgu, p, dg[:, p * SLOT : (p + 1) * SLOT])
            emit(pgu, tiles + p, du[:, p * SLOT : (p + 1) * SLOT])
        for p in range(2 * tiles, pgu.shape[0]):
            pgu[p] = jnp.zeros(pgu.shape[1:], bf16)
        d = dout.shape[1]
        for h in range(1, HQ):
            dout[h * HD : (h + 1) * HD] = dout[h * SLOT : h * SLOT + HD]
        for p in range(pout.shape[0]):
            size = min(SLOT, d - p * SLOT)
            value = dout[: HQ * HD, p * SLOT : p * SLOT + size]
            if size < SLOT:
                value = jnp.concatenate([value, jnp.zeros((HQ * HD, SLOT - size), f32)], axis=1)
            emit(pout, p, value)


def attn_bwd(tok, cs, gain, wqkv, q_in, k_in, v_in, mixed, xgrad, mgrad, igrad, pw, dgain, dpad, dw):
    @pl.when(pl.program_id(0) == 0)
    def _():
        dw[...] = jnp.zeros_like(dw)
        dgain[...] = jnp.zeros_like(dgain)

    lane = lax.broadcasted_iota(jnp.int32, (BLOCK, SLOT), 1)
    low = lane < HD
    table = cs[...]
    wide_seen = lax.broadcasted_iota(jnp.int32, (HALF, BLOCK), 0) <= lax.broadcasted_iota(jnp.int32, (HALF, BLOCK), 1)
    near_seen = wide_seen[:, :HALF]

    def group(g, carry):
        k = k_in[:, slot(g)]
        v = v_in[:, slot(g)]
        kt = k.astype(f32).T.astype(bf16)
        dk0 = dv0 = dk1 = dv1 = None
        for j in range(GROUPS):
            h = g * GROUPS + j
            q = q_in[:, slot(h)]
            go = xgrad[:, slot(h)].astype(f32)
            delta = jnp.sum(go * mixed[:, slot(h)].astype(f32), axis=1, keepdims=True)
            hi, mid, lo = split3(delta)
            go = jnp.where(lane == 64, -hi, go)
            go = jnp.where(lane == 65, -mid, go)
            go = jnp.where(lane == 66, -lo, go).astype(bf16)
            p0 = jnp.exp(jnp.where(wide_seen, dot_t(k[:HALF], q), FAR))
            s0 = (p0 * dot_t(v[:HALF], go)).astype(bf16)
            dv = dot(p0.astype(bf16), go)
            dk = dot(s0, q)
            dv0 = dv if dv0 is None else dv0 + dv
            dk0 = dk if dk0 is None else dk0 + dk
            p1 = jnp.exp(jnp.where(near_seen, dot_t(k[HALF:], q[HALF:]), FAR))
            s1 = (p1 * dot_t(v[HALF:], go[HALF:])).astype(bf16)
            dv = dot(p1.astype(bf16), go[HALF:])
            dk = dot(s1, q[HALF:])
            dv1 = dv if dv1 is None else dv1 + dv
            dk1 = dk if dk1 is None else dk1 + dk
            first = dot(kt[:, :HALF], s0)
            near = first[:, :HALF].T
            far = (first[:, HALF:] + dot(kt[:, HALF:], s1)).T
            dq = jnp.concatenate([near, far], axis=0) * (HD ** -0.5)
            dq = jnp.where(low, dq, 0.0)
            dpad[:, slot(h)] = ((dq + roll_half(dq)) * table).astype(bf16)
        dk = jnp.where(low, jnp.concatenate([dk0, dk1], axis=0), 0.0)
        dpad[:, slot(HQ + g)] = ((dk + roll_half(dk)) * table).astype(bf16)
        dv = jnp.where(low, jnp.concatenate([dv0, dv1], axis=0), 0.0)
        dpad[:, slot(HQ + KVH + g)] = dv.astype(bf16)
        return carry

    lax.fori_loop(0, KVH, group, 0)
    x = tok[...].astype(f32)
    inv = lax.rsqrt(jnp.mean(x * x, axis=1, keepdims=True) + EPS)
    nt = (x * inv * gain[...]).T.astype(bf16)
    dw[...] += dot(nt, dpad[...])
    part, gain_part = norm_back(dot_t(dpad[...], wqkv[...]), x, inv, gain[...])
    dgain[...] += gain_part
    igrad[...] = (mgrad[...] + part).astype(bf16)

    @pl.when(pl.program_id(0) == pl.num_programs(0) - 1)
    def _():
        d = dw.shape[0]
        lanes = lax.broadcasted_iota(jnp.int32, (d, SLOT), 1)

        def head(h):
            v = dw[:, h * SLOT : (h + 1) * SLOT]
            if h < HQ + KVH:
                v = v + jnp.where(lanes < HD // 2, pltpu.roll(v, HD // 2, 1), -pltpu.roll(v, SLOT - HD // 2, 1))
            return v

        heads = HQ + 2 * KVH
        for p in range(pw.shape[0]):
            v = jnp.where(lanes < HD, head(2 * p), 0.0)
            if 2 * p + 1 < heads:
                v = v + jnp.where(lanes < HD, 0.0, roll_half(head(2 * p + 1)))
            emit(pw, p, v)


def rows_spec(width):
    return pl.BlockSpec((BLOCK, width), lambda i: (i, 0))


def whole_spec(shape):
    return pl.BlockSpec(shape, lambda i: (0, 0), pipeline_mode=pl.Buffered(1))


def panel_spec(shape):
    return pl.BlockSpec(shape, lambda i: (0,) * len(shape), pipeline_mode=pl.Buffered(1))


def params():
    return pltpu.CompilerParams(vmem_limit_bytes=VMEM_BYTES, dimension_semantics=("arbitrary",))


def turned(w):
    half = HD // 2
    return jnp.concatenate([-w[..., half:], w[..., :half]], axis=-1)


def unturned(w):
    half = HD // 2
    return jnp.concatenate([w[..., half:], -w[..., :half]], axis=-1)


def tables_of(segments):
    rows = segments.shape[0]
    ids = segments.reshape(rows // BLOCK, BLOCK)
    index = jnp.arange(BLOCK, dtype=jnp.int32)
    earlier = jnp.concatenate([ids[:, :1] - 1, ids[:, :-1]], axis=1)
    starts = jnp.where(ids != earlier, index[None, :], 0)
    places = (index[None, :] - lax.cummax(starts, axis=1)).astype(f32).reshape(rows, 1)
    frequency = 100000.0 ** (jnp.arange(HD // 2, dtype=f32) * (-2.0 / HD))
    angles = places * frequency
    cosine, sine = jnp.cos(angles), jnp.sin(angles)
    return jnp.concatenate([cosine, cosine, sine, sine], axis=1)


def partner_of(me, bit):
    value = (me // 2**bit) % 2
    return value, me + (1 - 2 * value) * 2**bit


def greet(me, z, nbits, nshard):
    barrier = pltpu.get_barrier_semaphore()
    for bit in range(nbits):
        pl.semaphore_signal(
            barrier, inc=1, device_id=(partner_of(me, bit)[1], z), device_id_type=pl.DeviceIdType.MESH
        )
    for t in range(1, nshard):
        pl.semaphore_signal(
            barrier, inc=1, device_id=(me, (z + t) % nshard), device_id_type=pl.DeviceIdType.MESH
        )
    pl.semaphore_wait(barrier, nbits + nshard - 1)


def send(src, dst, sems, index, dp_id, z_id):
    copy = pltpu.make_async_remote_copy(
        src_ref=src,
        dst_ref=dst,
        send_sem=sems[0].at[index],
        recv_sem=sems[1].at[index],
        device_id=(dp_id, z_id),
        device_id_type=pl.DeviceIdType.MESH,
    )
    copy.start()
    return copy


def take_turns(chains):
    chains = list(chains)
    while chains:
        left = []
        for chain in chains:
            if next(chain, None) is not None:
                left.append(chain)
        chains = left


def gather_chain(order, me, z, nshard, w, full, sems):
    panels = w.shape[0]
    size, lo = panels, 0
    for bit in order:
        size //= 2
        lo = lo + partner_of(me, bit)[0] * size
    copies = []
    for t in range(1, nshard):
        copies.append(
            send(w.at[pl.ds(lo, size)], full.at[pl.ds(lo, size), z], sems, t - 1, me, (z + t) % nshard)
        )

    def own(i, carry):
        full[i, z] = w[i]
        return carry

    lax.fori_loop(0, panels, own, 0)
    yield True
    for copy in copies:
        copy.wait()
    used = nshard - 1
    for bit in reversed(order):
        value, partner = partner_of(me, bit)
        copies = []
        for t in range(1, nshard):
            part = full.at[pl.ds(lo, size), (z + t) % nshard]
            copies.append(send(part, part, sems, used + t - 1, partner, z))
        used += nshard - 1
        yield True
        for copy in copies:
            copy.wait()
        lo = lo - value * size
        size *= 2


def gather_kernel(orders, nshard, w0, w1, f0, f1, s0, r0, s1, r1):
    me, z = lax.axis_index("dp"), lax.axis_index("shard")
    greet(me, z, len(orders[0]), nshard)
    take_turns(
        [
            gather_chain(orders[0], me, z, nshard, w0, f0, (s0, r0)),
            gather_chain(orders[1], me, z, nshard, w1, f1, (s1, r1)),
        ]
    )


def reduce_chain(order, me, z, nshard, x, out, acc, recv, pieces, sems):
    size = x.shape[0]
    lo, place, landing = 0, 0, 0
    for k, bit in enumerate(order):
        size //= 2
        value, partner = partner_of(me, bit)
        source = x if k == 0 else acc
        copy = send(
            source.at[pl.ds(lo + (1 - value) * size, size)], recv.at[pl.ds(landing, size)], sems, k, partner, z
        )
        yield True
        copy.wait()
        keep = lo + value * size
        target = 0 if k == 0 else keep

        def add(i, carry, source=source, keep=keep, target=target, landing=landing):
            acc[target + i] = (source[keep + i].astype(f32) + recv[landing + i].astype(f32)).astype(bf16)
            return carry

        lax.fori_loop(0, size, add, 0)
        lo = target
        place = place + value * size
        landing += size
    used = len(order)
    copies = []
    for t in range(1, nshard):
        there = (z + t) % nshard
        copies.append(send(acc.at[pl.ds(lo, size), there], pieces.at[t - 1], sems, used + t - 1, me, there))
    used += nshard - 1
    yield True
    for copy in copies:
        copy.wait()
    for i in range(size):
        total = acc[lo + i, z].astype(f32)
        for t in range(1, nshard):
            total = total + pieces[t - 1, i].astype(f32)
        out[place + i] = total.astype(bf16)
    for bit in reversed(order):
        value, partner = partner_of(me, bit)
        part = out.at[pl.ds(place, size)]
        copy = send(part, part, sems, used, partner, z)
        used += 1
        yield True
        copy.wait()
        place = place - value * size
        size *= 2


def reduce_kernel(orders, nshard, x0, x1, o0, o1, a0, r0, p0, a1, r1, p1, s0, t0, s1, t1):
    me, z = lax.axis_index("dp"), lax.axis_index("shard")
    greet(me, z, len(orders[0]), nshard)
    take_turns(
        [
            reduce_chain(orders[0], me, z, nshard, x0, o0, a0, r0, p0, (s0, t0)),
            reduce_chain(orders[1], me, z, nshard, x1, o1, a1, r1, p1, (s1, t1)),
        ]
    )


def orders_of(ndp):
    bits = list(range(ndp.bit_length() - 1))
    return bits, bits[:1] + bits[:0:-1]


def whole_vmem():
    return pl.BlockSpec(memory_space=pltpu.VMEM)


def gather_panels(ndp, nshard, w0, w1):
    rows = w0.shape[1]
    orders = orders_of(ndp)
    count = (nshard - 1) * (1 + len(orders[0]))
    return pl.pallas_call(
        functools.partial(gather_kernel, orders, nshard),
        in_specs=[whole_vmem()] * 2,
        out_specs=[whole_vmem()] * 2,
        out_shape=[jax.ShapeDtypeStruct((w.shape[0], nshard, rows, SLOT), bf16) for w in (w0, w1)],
        scratch_shapes=[pltpu.SemaphoreType.DMA((count,))] * 4,
        compiler_params=pltpu.CompilerParams(
            collective_id=0, has_side_effects=True, vmem_limit_bytes=VMEM_BYTES
        ),
        name="gather_panels",
    )(w0, w1)


def reduce_panels(ndp, nshard, x0, x1):
    rows = x0.shape[2]
    orders = orders_of(ndp)
    count = 2 * len(orders[0]) + nshard - 1
    scratch = []
    for x in (x0, x1):
        n = x.shape[0]
        scratch += [
            pltpu.VMEM((n // 2, nshard, rows, SLOT), bf16),
            pltpu.VMEM((n, nshard, rows, SLOT), bf16),
            pltpu.VMEM((nshard - 1, n // ndp, rows, SLOT), bf16),
        ]
    return pl.pallas_call(
        functools.partial(reduce_kernel, orders, nshard),
        in_specs=[whole_vmem()] * 2,
        out_specs=[whole_vmem()] * 2,
        out_shape=[jax.ShapeDtypeStruct((x.shape[0], rows, SLOT), bf16) for x in (x0, x1)],
        scratch_shapes=scratch + [pltpu.SemaphoreType.DMA((count,))] * 4,
        compiler_params=pltpu.CompilerParams(
            collective_id=1, has_side_effects=True, vmem_limit_bytes=VMEM_BYTES
        ),
        name="reduce_panels",
    )(x0, x1)


def to_panels(w, ndp):
    rows, columns = w.shape
    count = -(-columns // (SLOT * ndp)) * ndp
    w = jnp.pad(w, ((0, 0), (0, count * SLOT - columns)))
    return w.reshape(rows, count, SLOT).transpose(1, 0, 2)


def from_panels(p):
    return p.transpose(1, 0, 2).reshape(p.shape[1], -1)


def gather_weights(ndp, norm_attn, w_query, w_key, w_value, w_out, norm_ffn, w_gate, w_up, w_down):
    rows = norm_attn.shape[0]
    ff, d = w_gate.shape[1], w_query.shape[1]
    gains = jnp.concatenate(
        [norm_attn[:, None], norm_ffn[:, None], jnp.zeros((rows, HD - 2), bf16)], axis=1
    )
    down = w_down.reshape(rows, -1)
    first = to_panels(jnp.concatenate([w_gate, w_up], axis=1), ndp)
    second = to_panels(jnp.concatenate([down, w_query, w_key, w_value, w_out, gains], axis=1), ndp)
    first, second = gather_panels(ndp, d // rows, first, second)
    first = first.reshape(-1, d, SLOT)
    full = from_panels(second.reshape(-1, d, SLOT))
    wdown = full[:, :ff].reshape(ff, d)
    at = ff
    qk = full[:, at : at + (HQ + KVH) * HD]
    at += (HQ + KVH) * HD
    wv = full[:, at : at + KVH * HD]
    at += KVH * HD
    wout = full[:, at : at + d]
    at += d
    gain_one = full[:, at].astype(f32)[None, :]
    gain_two = full[:, at + 1].astype(f32)[None, :]
    return first, qk, wv, wout, gain_one, gain_two, wdown


def shards(ndp, tokens, segments, norm_attn, w_query, w_key, w_value, w_out, norm_ffn, w_gate, w_up, w_down, cotangent):
    rows, d = tokens.shape
    ff = w_gate.shape[1]
    nshard = d // norm_attn.shape[0]
    grid = (rows // BLOCK,)
    gu, qk, wv, wout, gain_one, gain_two, wdown = gather_weights(
        ndp, norm_attn, w_query, w_key, w_value, w_out, norm_ffn, w_gate, w_up, w_down
    )
    qk = qk.reshape(d, HQ + KVH, HD)
    qk = jnp.concatenate([qk, turned(qk)], axis=-1).reshape(d, -1)
    wv = jnp.pad(wv.reshape(d, KVH, HD), ((0, 0), (0, 0), (0, SLOT - HD))).reshape(d, -1)
    wqkv = jnp.concatenate([qk, wv], axis=1)
    wout = jnp.pad(wout.reshape(HQ, HD, d), ((0, 0), (0, SLOT - HD), (0, 0))).reshape(HQ * SLOT, d)
    cs = tables_of(segments)
    seg = segments[:, None]
    qw, kw, allw = HQ * SLOT, KVH * SLOT, (HQ + 2 * KVH) * SLOT
    shape = jax.ShapeDtypeStruct

    q, k, v, mixed = pl.pallas_call(
        attn_fwd,
        grid=grid,
        in_specs=[rows_spec(d), rows_spec(SLOT), rows_spec(1), whole_spec((1, d)), whole_spec((d, allw))],
        out_specs=[rows_spec(qw), rows_spec(kw), rows_spec(kw), rows_spec(qw)],
        out_shape=[shape((rows, qw), bf16), shape((rows, kw), bf16), shape((rows, kw), bf16), shape((rows, qw), bf16)],
        compiler_params=params(),
        name="attn_fwd",
    )(tokens, cs, seg, gain_one, wqkv)

    own = (nshard, d // nshard, SLOT)
    out_panels, qkv_panels = -(-d // SLOT), (HQ + 2 * KVH + 1) // 2
    output, mgrad, xgrad, pout, pgu, dd, dgain_two = pl.pallas_call(
        ffn,
        grid=grid,
        in_specs=[
            rows_spec(d), rows_spec(qw), rows_spec(d), whole_spec((1, d)), whole_spec((qw, d)),
            panel_spec(gu.shape), whole_spec((ff, d)),
        ],
        out_specs=[
            rows_spec(d), rows_spec(d), rows_spec(qw), panel_spec((out_panels,) + own),
            panel_spec((gu.shape[0],) + own), whole_spec((d, ff)), whole_spec((1, d)),
        ],
        out_shape=[
            shape((rows, d), bf16), shape((rows, d), f32), shape((rows, qw), bf16), shape((out_panels,) + own, bf16),
            shape((gu.shape[0],) + own, bf16), shape((d, ff), f32), shape((1, d), f32),
        ],
        scratch_shapes=[
            pltpu.VMEM((BLOCK, d), bf16), pltpu.VMEM((d, BLOCK), bf16), pltpu.VMEM((d, BLOCK), bf16),
            pltpu.VMEM((BLOCK, d), f32), pltpu.VMEM((BLOCK, d), f32),
            pltpu.VMEM((d, ff), bf16), pltpu.VMEM((d, ff), bf16), pltpu.VMEM((d, ff), f32), pltpu.VMEM((d, ff), f32),
            pltpu.VMEM((qw, d), f32),
        ],
        compiler_params=params(),
        name="ffn",
    )(tokens, mixed, cotangent, gain_two, wout, gu, wdown)

    igrad, pw, dgain_one = pl.pallas_call(
        attn_bwd,
        grid=grid,
        in_specs=[
            rows_spec(d), rows_spec(SLOT), whole_spec((1, d)), whole_spec((d, allw)), rows_spec(qw),
            rows_spec(kw), rows_spec(kw), rows_spec(qw), rows_spec(qw), rows_spec(d),
        ],
        out_specs=[rows_spec(d), panel_spec((qkv_panels,) + own), whole_spec((1, d))],
        out_shape=[shape((rows, d), bf16), shape((qkv_panels,) + own, bf16), shape((1, d), f32)],
        scratch_shapes=[pltpu.VMEM((BLOCK, allw), bf16), pltpu.VMEM((d, allw), f32)],
        compiler_params=params(),
        name="attn_bwd",
    )(tokens, cs, gain_one, wqkv, q, k, v, mixed, xgrad, mgrad)

    own_ff = ff // nshard
    dd = dd.reshape(d, nshard, own_ff).transpose(1, 0, 2).reshape(nshard * own_ff, d)
    dd = dd.reshape(d, ff)
    gains = jnp.pad(jnp.concatenate([dgain_one.T, dgain_two.T], axis=1), ((0, 0), (0, SLOT - 2)))
    dd = to_panels(dd.astype(bf16), 1).reshape((-1,) + own)
    gains = gains.astype(bf16).reshape((1,) + own)
    filled = dd.shape[0] + out_panels + qkv_panels + 1
    rest = jnp.zeros((-filled % ndp,) + own, bf16)
    second = jnp.concatenate([dd, pw, pout, gains, rest], axis=0)
    first = pgu
    first, second = reduce_panels(ndp, nshard, first, second)
    first = from_panels(first).astype(f32)
    second = from_panels(second).astype(f32)
    down = second[:, :ff].reshape(d, ff // nshard).T
    nq, nk = HQ * HD, KVH * HD
    second = second[:, ff:]
    at = nq + 2 * nk
    start = qkv_panels * SLOT
    gain_at = start + out_panels * SLOT
    return (
        output,
        igrad,
        second[:, gain_at],
        second[:, :nq],
        second[:, nq : nq + nk],
        second[:, nq + nk : at],
        second[:, start : start + d],
        second[:, gain_at + 1],
        first[:, :ff],
        first[:, ff : 2 * ff],
        down,
    )


def solution(mesh):
    rows = P(("dp", "shard"), None)
    weight, gain = P("shard", None), P("shard")
    in_specs = (
        rows, P(("dp", "shard")), gain, weight, weight, weight, weight, gain, weight, weight, weight, rows
    )
    out_specs = (rows, rows, gain, weight, weight, weight, weight, gain, weight, weight, weight)
    return jax.shard_map(functools.partial(shards, mesh.shape["dp"]), mesh=mesh, in_specs=in_specs, out_specs=out_specs, check_vma=False)
```
